32 devices in a mesh: groups: 2 (over y), row: 4 (over z), tm: 2 (over x), chan: 2 (over core).
Axes of the slice: x: 2, y: 2, z: 4, core: 2. Of those that a mesh axis runs over, the one named last changes fastest.
Arguments:
- field_in: bfloat16 [64, 8, 128, 128], P(('groups', 'row'), 'tm', 'chan'), parts along dimension 0, may hold values from -6 to 6
- spectral_weight: bfloat16 [8, 32, 32, 2, 128, 128], P('tm', 'row', None, None, 'chan'), may hold values from -0.75 to 0.75
- conv_weight: bfloat16 [128, 128], P('chan'), may hold values from -0.5 to 0.5
- conv_bias: float32 [128], P('chan'), may hold values from -3 to 3
Outputs:
- layer_out: bfloat16 [64, 8, 128, 128], P(('groups', 'row'), 'tm', 'chan'), parts along dimension 0
The draws below stay inside these ranges and needn't reach their ends.
There are 2 independent parts, one for each index of `groups`. The reference program is written for one: setup_inputs(seed, part) draws one part's arguments, and reference() takes and returns one part's arrays. A program takes and returns all parts, laid end to end along the dimension named above; an argument that names none is the same for every part. Nothing has to cross between parts.
All inputs are finite; a program needn't handle non-finite values.
Results may differ from the reference program's by a relative error of at most 0.007.
Values may be sent and summed in bfloat16 or wider, within the bound.
A program may use at most 128 MiB of HBM per device.

```python
import math
import jax
import jax.numpy as jnp
from jax import lax

C = 128
KX = 32
KY = 32
KT = 8
NX = 128
NY = 32
NT = 8
MODES = 8192


def block_scale(own_key, shape, cuts, least, top_value):
    def one(axis_at, parts):
        draws = jax.random.uniform(jax.random.fold_in(jax.random.fold_in(own_key, 6), axis_at), (parts,), jnp.float32, least / len(cuts), top_value / len(cuts))
        return jnp.repeat(jnp.exp(draws), shape[axis_at] // parts).reshape((-1,) + (1,) * (len(shape) - axis_at - 1))

    loudness = one(*cuts[0])
    for cut in cuts[1:]:
        loudness = loudness * one(*cut)
    return loudness


def noise(stream_key, dims, deviation, bound, shards=(), kind=jnp.bfloat16):
    values = jax.random.normal(stream_key, dims, jnp.float32) * deviation
    if len(shards) > 0:
        values = block_scale(stream_key, dims, shards, -0.22, 0.18) * values
    return jnp.clip(values, min=-bound, max=bound).astype(kind)


def setup_inputs(seed: int = 0, part: int = 0) -> dict:
    streams_of = jax.random.split(jax.random.key(seed), 5)
    part_keys = jax.random.split(jax.random.fold_in(streams_of[4], part), 5)
    field_in = noise(part_keys[0], (NY, NT, C, NX), 1.0, 6.0, ((0, 4), (1, 2), (2, 2)))
    spectral_weight = noise(streams_of[1], (KT, KY, KX, 2, C, C), (max(1, 2 * MODES * C // (NX * NY * NT))) ** -0.5, 0.75, ((0, 2), (1, 4), (4, 2)))
    conv_weight = noise(streams_of[2], (C, C), C ** -0.5, 0.5, ((0, 2),))
    conv_bias = noise(streams_of[3], (C,), 0.5, 3.0, ((0, 2),), jnp.float32)
    return {"field_in": field_in, "spectral_weight": spectral_weight, "conv_weight": conv_weight, "conv_bias": conv_bias}


def phase_table(position, frequency, period):
    turns = jnp.mod(position * frequency, period).astype(jnp.float32) * (2.0 * math.pi / period)
    return jnp.cos(turns), jnp.sin(turns)


def signed(index_list, total):
    return jnp.where(index_list < total // 2, index_list, index_list - total)


def rotate(values, cos_table, sin_table, formula, orient):
    cos_part = jnp.einsum(formula, values, cos_table, precision=lax.Precision.HIGHEST)
    sin_part = jnp.einsum(formula, values, sin_table, precision=lax.Precision.HIGHEST)
    real_part = cos_part[..., 0, :] - orient * sin_part[..., 1, :]
    imag_part = cos_part[..., 1, :] + orient * sin_part[..., 0, :]
    return jnp.stack([real_part, imag_part], axis=-2)


def mix_modes(coefficients, weights):
    coeff_f = coefficients.astype(jnp.float32)
    weight_f = weights.astype(jnp.float32)
    real_w = weight_f[:, :, :, 0]
    imag_w = weight_f[:, :, :, 1]
    real_c = coeff_f[:, :, :, 0]
    imag_c = coeff_f[:, :, :, 1]

    def product(left, right):
        return jnp.einsum("baxoi,baix->baox", left, right, precision=lax.Precision.HIGHEST)

    real_part = product(real_w, real_c) - product(imag_w, imag_c)
    imag_part = product(real_w, imag_c) + product(imag_w, real_c)
    return jnp.stack([real_part, imag_part], axis=3)


def reference(field_in, spectral_weight, conv_weight, conv_bias):
    x_pos = jnp.arange(NX, dtype=jnp.int32)
    y_pos = jnp.arange(NY, dtype=jnp.int32)
    t_pos = jnp.arange(NT, dtype=jnp.int32)
    kx_list = jnp.arange(KX, dtype=jnp.int32)
    ky_list = signed(jnp.arange(KY, dtype=jnp.int32), KY)
    kt_list = signed(jnp.arange(KT, dtype=jnp.int32), KT)
    cos_f, sin_f = phase_table(x_pos[:, None], kx_list[None, :], NX)
    x_table = jnp.stack([cos_f, -sin_f], axis=1).astype(jnp.bfloat16)
    section_x = jnp.einsum("ytcn,npx->ytcpx", field_in.astype(jnp.float32), x_table.astype(jnp.float32), precision=lax.Precision.HIGHEST)
    cos_y, sin_y = phase_table(y_pos[:, None], ky_list[None, :], NY)
    section_y = rotate(section_x, cos_y, sin_y, "ytcpx,yk->ktcpx", -1.0)
    cos_t, sin_t = phase_table(t_pos[:, None], kt_list[None, :], NT)
    coefficients = rotate(section_y, cos_t, sin_t, "ktcpx,tb->bkcpx", -1.0).astype(jnp.bfloat16)
    mixed_modes = mix_modes(coefficients, spectral_weight).astype(jnp.bfloat16)
    back_cos_t, back_sin_t = phase_table(kt_list[:, None], t_pos[None, :], NT)
    back_t = rotate(mixed_modes.astype(jnp.float32), back_cos_t, back_sin_t, "bkcpx,bt->ktcpx", 1.0)
    back_cos_y, back_sin_y = phase_table(ky_list[:, None], y_pos[None, :], NY)
    back_y = rotate(back_t, back_cos_y, back_sin_y, "ktcpx,ky->ytcpx", 1.0)
    cos_x, sin_x = phase_table(kx_list[:, None], x_pos[None, :], NX)
    scale = jnp.where(kx_list == 0, 1.0, 2.0).astype(jnp.float32) / float(NX * NY * NT)
    inverse_x = jnp.stack([cos_x * scale[:, None], -sin_x * scale[:, None]], axis=0)
    spectral = jnp.einsum("ytcpx,pxn->ytcn", back_y, inverse_x, precision=lax.Precision.HIGHEST)
    conv = jnp.einsum("oi,ytin->yton", conv_weight.astype(jnp.float32), field_in.astype(jnp.float32), precision=lax.Precision.HIGHEST)
    summed = spectral + conv + conv_bias[None, None, :, None]
    return jax.nn.gelu(summed, approximate=False).astype(jnp.bfloat16)
```

```python
import functools

import jax
import jax.numpy as jnp
import numpy as np
from jax import lax
from jax.experimental import pallas as pl
from jax.experimental.pallas import tpu as pltpu
from jax.sharding import PartitionSpec as P

MESH = pl.DeviceIdType.MESH
F32 = jnp.float32
BF16 = jnp.bfloat16


def angles(frequency, position, period):
    return 2.0 * np.pi * np.mod(np.outer(frequency, position), period) / period


def signed(count):
    index = np.arange(count)
    return np.where(index < count // 2, index, index - count)


def swap_halves(value):
    return pltpu.roll(value, 64, axis=value.ndim - 1)


def kernel(
    dims,
    field,
    weights,
    conv_w,
    bias,
    x_fwd,
    x_inv,
    tab_y,
    tab_t,
    out,
    w_all,
    f_all,
    sect,
    sect_s,
    y_send,
    y_recv,
    own_kt,
    t_send,
    t_recv,
    coef,
    modes,
    back,
    acc,
    conv,
    w_sem,
    f_sem,
    fs_sem,
    fr_sem,
    ys_sem,
    yr_sem,
    ts_sem,
    tr_sem,
    cs_sem,
    cr_sem,
    ms_sem,
    mr_sem,
    bs_sem,
    br_sem,
):
    rows, slabs, yd, td, kyd, ktd, kx = dims
    ky_all, kt_all = rows * kyd, slabs * ktd
    row, tm, chan = lax.axis_index("row"), lax.axis_index("tm"), lax.axis_index("chan")
    y0, t0 = row * yd, tm * td
    half = 64

    barrier = pltpu.get_barrier_semaphore()
    for d in range(1, rows):
        pl.semaphore_signal(
            barrier, inc=1, device_id={"row": lax.rem(row + d, rows)}, device_id_type=MESH
        )
    for d in range(1, slabs):
        pl.semaphore_signal(
            barrier, inc=1, device_id={"tm": lax.rem(tm + d, slabs)}, device_id_type=MESH
        )
    pl.semaphore_signal(barrier, inc=1, device_id={"chan": 1 - chan}, device_id_type=MESH)

    mine = pl.ds(pl.multiple_of(chan * half, half), half)
    own_field = pltpu.make_async_copy(field, f_all.at[:, mine, :], f_sem)
    own_field.start()
    w_copies = [
        pltpu.make_async_copy(weights.at[b], w_all.at[b], w_sem.at[b]) for b in range(ktd)
    ]
    for copy in w_copies:
        copy.start()

    lane = lax.broadcasted_iota(jnp.int32, (kx, 128), 1)
    low = lane < half
    sgn_f = jnp.where(low, 1.0, -1.0).astype(F32)
    low8 = low[:8]
    sgn_b = -sgn_f

    own_field.wait()

    def x_step(i, carry):
        block = f_all[pl.ds(2 * i, 2), mine, :].reshape(2 * half, 128)
        both = lax.dot_general(
            x_fwd[...], block, (((1,), (1,)), ((), ())), preferred_element_type=F32
        )
        re, im = both[:kx], both[kx:]
        first = jnp.where(low, re, swap_halves(im))
        second = jnp.where(low, swap_halves(re), im)
        sect[2 * i] = first
        sect_s[2 * i] = swap_halves(first) * sgn_f
        sect[2 * i + 1] = second
        sect_s[2 * i + 1] = swap_halves(second) * sgn_f
        return carry

    lax.fori_loop(0, yd * td // 2, x_step, 0)

    pl.semaphore_wait(barrier, rows - 1 + slabs - 1 + 1)
    pending = []

    y_recvs = []
    for d in list(range(1, rows)) + [0]:
        dest = lax.rem(row + d, rows)

        def y_step(a, carry, d=d, dest=dest):
            k = dest * kyd + a
            for t in range(td):
                total = jnp.zeros((kx, 128), F32)
                for y in range(yd):
                    total += tab_y[k, y0 + y] * sect[y * td + t]
                    total += tab_y[ky_all + k, y0 + y] * sect_s[y * td + t]
                if d == 0:
                    y_recv[row, a, t] = total.astype(BF16)
                else:
                    y_send[d - 1, a, t] = total.astype(BF16)
            return carry

        lax.fori_loop(0, kyd, y_step, 0)
        if d > 0:
            copy = pltpu.make_async_remote_copy(
                src_ref=y_send.at[d - 1],
                dst_ref=y_recv.at[row],
                send_sem=ys_sem.at[d - 1],
                recv_sem=yr_sem.at[d - 1],
                device_id={"row": dest},
                device_id_type=MESH,
            )
            copy.start()
            pending.append(copy)
            y_recvs.append(copy)

    f_copy = pltpu.make_async_remote_copy(
        src_ref=field,
        dst_ref=f_all.at[:, mine, :],
        send_sem=fs_sem,
        recv_sem=fr_sem,
        device_id={"chan": 1 - chan},
        device_id_type=MESH,
    )
    f_copy.start()
    pending.append(f_copy)
    f_copy.wait_recv()

    def conv_step(i, carry):
        conv[i] = jnp.dot(conv_w[...], f_all[i], preferred_element_type=F32) + bias[...]
        return carry

    lax.fori_loop(0, yd * td, conv_step, 0)

    for copy in y_recvs:
        copy.wait_recv()

    def t_step(a, carry):
        parts = []
        for t in range(td):
            total = y_recv[0, a, t].astype(F32)
            for r in range(1, rows):
                total += y_recv[r, a, t].astype(F32)
            parts.append((total, swap_halves(total) * sgn_f))
        for d in range(slabs):
            dest = lax.rem(tm + d, slabs)
            for b in range(ktd):
                k = dest * ktd + b
                value = jnp.zeros((kx, 128), F32)
                for t in range(td):
                    value += tab_t[k, t0 + t] * parts[t][0]
                    value += tab_t[kt_all + k, t0 + t] * parts[t][1]
                if d == 0:
                    own_kt[b, a] = value
                else:
                    t_send[d - 1, b, a] = value.astype(BF16)
        return carry

    lax.fori_loop(0, kyd, t_step, 0)
    t_copies = []
    for d in range(1, slabs):
        copy = pltpu.make_async_remote_copy(
            src_ref=t_send.at[d - 1],
            dst_ref=t_recv.at[d - 1],
            send_sem=ts_sem.at[d - 1],
            recv_sem=tr_sem.at[d - 1],
            device_id={"tm": lax.rem(tm + d, slabs)},
            device_id_type=MESH,
        )
        copy.start()
        t_copies.append(copy)
        pending.append(copy)
    for copy in t_copies:
        copy.wait_recv()

    for b in range(ktd):

        def c_step(a, carry, b=b):
            value = own_kt[b, a]
            for d in range(1, slabs):
                value += t_recv[d - 1, b, a].astype(F32)
            coef[chan, b, a] = value.astype(BF16)
            return carry

        lax.fori_loop(0, kyd, c_step, 0)
    c_copy = pltpu.make_async_remote_copy(
        src_ref=coef.at[chan],
        dst_ref=coef.at[chan],
        send_sem=cs_sem,
        recv_sem=cr_sem,
        device_id={"chan": 1 - chan},
        device_id_type=MESH,
    )
    c_copy.start()
    pending.append(c_copy)
    c_copy.wait_recv()

    group = 8 * 2 * half
    sub = lax.broadcasted_iota(jnp.int32, (8, 128), 0)
    zero = jnp.zeros((8, 128), F32)
    m_copies = []
    for b in range(ktd):
        w_copies[b].wait()
        kt = tm * ktd + b

        def mix_step(a, carry, b=b, kt=kt):
            left = coef[0, b, a].astype(F32)
            right = coef[1, b, a].astype(F32)
            re = jnp.where(low, left, swap_halves(right))
            im = jnp.where(low, swap_halves(left), right)
            pieces = []
            for g in range(0, kx // 8, 2):
                first, second = slice(8 * g, 8 * g + 8), slice(8 * g + 8, 8 * g + 16)
                lhs = jnp.concatenate(
                    [
                        jnp.concatenate([re[first], zero], axis=1),
                        jnp.concatenate([im[first], zero], axis=1),
                        jnp.concatenate([zero, re[second]], axis=1),
                        jnp.concatenate([zero, im[second]], axis=1),
                    ],
                    axis=0,
                ).astype(BF16)
                rhs = jnp.concatenate(
                    [
                        w_all[b, a, g * group : (g + 1) * group, :],
                        w_all[b, a, (g + 1) * group : (g + 2) * group, :],
                    ],
                    axis=1,
                )
                result = lax.dot_general(
                    lhs, rhs, (((1,), (1,)), ((), ())), preferred_element_type=F32
                )
                for h in range(2):
                    by_part = []
                    for p in range(2):
                        tile = result[16 * h + 8 * p : 16 * h + 8 * p + 8]
                        total = tile[:, :128]
                        for m in range(1, 8):
                            total = jnp.where(sub == m, tile[:, 128 * m : 128 * m + 128], total)
                        by_part.append(total)
                    turned = swap_halves(by_part[1])
                    pieces.append(by_part[0] + jnp.where(low8, -turned, turned))
            modes[kt, a] = jnp.concatenate(pieces, axis=0).astype(BF16)
            return carry

        lax.fori_loop(0, kyd, mix_step, 0)
        for d in range(1, slabs):
            copy = pltpu.make_async_remote_copy(
                src_ref=modes.at[kt],
                dst_ref=modes.at[kt],
                send_sem=ms_sem.at[d - 1, b],
                recv_sem=mr_sem.at[d - 1, b],
                device_id={"tm": lax.rem(tm + d, slabs)},
                device_id_type=MESH,
            )
            copy.start()
            m_copies.append(copy)
            pending.append(copy)
    for copy in m_copies:
        copy.wait_recv()

    def bt_step(a, carry):
        totals = [jnp.zeros((kx, 128), F32) for _ in range(td)]
        for k in range(kt_all):
            value = modes[k, a].astype(F32)
            turned = swap_halves(value) * sgn_b
            for t in range(td):
                totals[t] += tab_t[k, t0 + t] * value + tab_t[kt_all + k, t0 + t] * turned
        for t in range(td):
            back[row, a, t] = totals[t].astype(BF16)
        return carry

    lax.fori_loop(0, kyd, bt_step, 0)
    b_copies = []
    for d in range(1, rows):
        copy = pltpu.make_async_remote_copy(
            src_ref=back.at[row],
            dst_ref=back.at[row],
            send_sem=bs_sem.at[d - 1],
            recv_sem=br_sem.at[d - 1],
            device_id={"row": lax.rem(row + d, rows)},
            device_id_type=MESH,
        )
        copy.start()
        b_copies.append(copy)
        pending.append(copy)

    for d in range(rows):
        source = lax.rem(row - d + rows, rows)
        if d > 0:
            b_copies[d - 1].wait_recv()

        def by_step(t, carry, d=d, source=source):
            if d == 0:
                totals = [jnp.zeros((kx, 128), F32) for _ in range(yd)]
            else:
                totals = [acc[y * td + t] for y in range(yd)]
            for a in range(kyd):
                k = source * kyd + a
                value = back[source, a, t].astype(F32)
                turned = swap_halves(value) * sgn_b
                for y in range(yd):
                    totals[y] += (
                        tab_y[k, y0 + y] * value + tab_y[ky_all + k, y0 + y] * turned
                    )
            for y in range(yd):
                acc[y * td + t] = totals[y]
            return carry

        lax.fori_loop(0, td, by_step, 0)

    def out_step(i, carry):
        first, second = acc[2 * i], acc[2 * i + 1]
        both = jnp.concatenate(
            [
                jnp.where(low, first, swap_halves(second)),
                jnp.where(low, swap_halves(first), second),
            ],
            axis=0,
        )
        spectral = jnp.dot(both.T.astype(BF16), x_inv[...], preferred_element_type=F32)
        value = spectral + conv[pl.ds(2 * i, 2)].reshape(2 * half, 128)
        value = 0.5 * value * (1.0 + lax.erf(value * np.float32(1.0 / np.sqrt(2.0))))
        out[pl.ds(2 * i, 2)] = value.astype(BF16).reshape(2, half, 128)
        return carry

    lax.fori_loop(0, yd * td // 2, out_step, 0)
    for copy in pending:
        copy.wait_send()


def body(field_in, spectral_weight, conv_weight, conv_bias):
    yd, td, half, nx = field_in.shape
    ktd, kyd, kx = spectral_weight.shape[:3]
    out_c, in_c = spectral_weight.shape[4:]
    rows, slabs = lax.axis_size("row"), lax.axis_size("tm")
    ny, nt = yd * rows, td * slabs
    ky_all, kt_all = kyd * rows, ktd * slabs

    turn_x = angles(np.arange(kx), np.arange(nx), nx)
    x_fwd = jnp.asarray(np.concatenate([np.cos(turn_x), -np.sin(turn_x)], axis=0), BF16)
    scale = (np.where(np.arange(kx) == 0, 1.0, 2.0) / (nx * ny * nt))[:, None]
    x_inv = jnp.asarray(
        np.concatenate([np.cos(turn_x) * scale, -np.sin(turn_x) * scale], axis=0), BF16
    )
    turn_y = angles(signed(ky_all), np.arange(ny), ny)
    tab_y = jnp.asarray(np.concatenate([np.cos(turn_y), np.sin(turn_y)], axis=0), F32)
    turn_t = angles(signed(kt_all), np.arange(nt), nt)
    tab_t = jnp.asarray(np.concatenate([np.cos(turn_t), np.sin(turn_t)], axis=0), F32)

    dims = (rows, slabs, yd, td, kyd, ktd, kx)
    vmem = pl.BlockSpec(memory_space=pltpu.VMEM)
    smem = pl.BlockSpec(memory_space=pltpu.SMEM)
    hbm = pl.BlockSpec(memory_space=pl.ANY)
    dma = pltpu.SemaphoreType.DMA
    tile = (kx, 128)
    result = pl.pallas_call(
        functools.partial(kernel, dims),
        out_shape=jax.ShapeDtypeStruct((yd * td, half, nx), BF16),
        in_specs=[hbm, hbm, vmem, vmem, vmem, vmem, smem, smem],
        out_specs=vmem,
        scratch_shapes=[
            pltpu.VMEM((ktd, kyd, kx * 2 * out_c, in_c), BF16),
            pltpu.VMEM((yd * td, in_c, nx), BF16),
            pltpu.VMEM((yd * td,) + tile, F32),
            pltpu.VMEM((yd * td,) + tile, F32),
            pltpu.VMEM((rows - 1, kyd, td) + tile, BF16),
            pltpu.VMEM((rows, kyd, td) + tile, BF16),
            pltpu.VMEM((ktd, kyd) + tile, F32),
            pltpu.VMEM((slabs - 1, ktd, kyd) + tile, BF16),
            pltpu.VMEM((slabs - 1, ktd, kyd) + tile, BF16),
            pltpu.VMEM((2, ktd, kyd) + tile, BF16),
            pltpu.VMEM((kt_all, kyd) + tile, BF16),
            pltpu.VMEM((rows, kyd, td) + tile, BF16),
            pltpu.VMEM((yd * td,) + tile, F32),
            pltpu.VMEM((yd * td, out_c, nx), F32),
            dma((ktd,)),
            dma,
            dma,
            dma,
            dma((rows - 1,)),
            dma((rows - 1,)),
            dma((slabs - 1,)),
            dma((slabs - 1,)),
            dma,
            dma,
            dma((slabs - 1, ktd)),
            dma((slabs - 1, ktd)),
            dma((rows - 1,)),
            dma((rows - 1,)),
        ],
        compiler_params=pltpu.CompilerParams(
            collective_id=0, has_side_effects=True, vmem_limit_bytes=56 * 1024 * 1024
        ),
    )(
        field_in.reshape(yd * td, half, nx),
        spectral_weight.reshape(ktd, kyd, kx * 2 * out_c, in_c),
        conv_weight,
        conv_bias[:, None],
        x_fwd,
        x_inv,
        tab_y,
        tab_t,
    )
    return result.reshape(yd, td, half, nx)


def solution(mesh):
    return jax.shard_map(
        body,
        mesh=mesh,
        in_specs=(
            P(("groups", "row"), "tm", "chan", None),
            P("tm", "row", None, None, "chan", None),
            P("chan", None),
            P("chan"),
        ),
        out_specs=P(("groups", "row"), "tm", "chan", None),
        check_vma=False,
    )
```

```python
import functools

import jax
import jax.numpy as jnp
import numpy as np
from jax import lax
from jax.experimental import pallas as pl
from jax.experimental.pallas import tpu as pltpu
from jax.sharding import PartitionSpec as P

MESH = pl.DeviceIdType.MESH
F32 = jnp.float32
BF16 = jnp.bfloat16


def angles(frequency, position, period):
    return 2.0 * np.pi * np.mod(np.outer(frequency, position), period) / period


def signed(count):
    index = np.arange(count)
    return np.where(index < count // 2, index, index - count)


def swap_halves(value):
    return pltpu.roll(value, 64, axis=value.ndim - 1)


def kernel(
    dims,
    field,
    weights,
    conv_w,
    bias,
    x_fwd,
    x_inv,
    tab_y,
    tab_t,
    out,
    w_all,
    f_all,
    sect,
    sect_s,
    y_send,
    y_recv,
    own_kt,
    t_send,
    t_recv,
    coef,
    modes,
    back,
    acc,
    conv,
    w_sem,
    f_sem,
    fs_sem,
    fr_sem,
    ys_sem,
    yr_sem,
    ts_sem,
    tr_sem,
    cs_sem,
    cr_sem,
    ms_sem,
    mr_sem,
    bs_sem,
    br_sem,
):
    rows, slabs, yd, td, kyd, ktd, kx, parts = dims
    ky_all, kt_all = rows * kyd, slabs * ktd
    row, tm, chan = lax.axis_index("row"), lax.axis_index("tm"), lax.axis_index("chan")
    y0, t0 = row * yd, tm * td
    half = 64

    barrier = pltpu.get_barrier_semaphore()
    for d in range(1, rows):
        pl.semaphore_signal(
            barrier, inc=1, device_id={"row": lax.rem(row + d, rows)}, device_id_type=MESH
        )
    for d in range(1, slabs):
        pl.semaphore_signal(
            barrier, inc=1, device_id={"tm": lax.rem(tm + d, slabs)}, device_id_type=MESH
        )
    pl.semaphore_signal(barrier, inc=1, device_id={"chan": 1 - chan}, device_id_type=MESH)

    mine = pl.ds(pl.multiple_of(chan * half, half), half)
    own_field = pltpu.make_async_copy(field, f_all.at[:, mine, :], f_sem)
    own_field.start()
    span = max(1, kyd // parts)
    count = kyd // span
    part = [pl.ds(c * span, span) for c in range(count)]
    w_copies = [
        pltpu.make_async_copy(weights.at[:, part[c]], w_all.at[:, part[c]], w_sem.at[c])
        for c in range(count)
    ]
    for copy in w_copies:
        copy.start()

    lane = lax.broadcasted_iota(jnp.int32, (kx, 128), 1)
    low = lane < half
    sgn_f = jnp.where(low, 1.0, -1.0).astype(F32)
    low8 = low[:8]
    sgn_b = -sgn_f

    own_field.wait()

    def x_step(i, carry):
        block = f_all[pl.ds(2 * i, 2), mine, :].reshape(2 * half, 128)
        both = lax.dot_general(
            x_fwd[...], block, (((1,), (1,)), ((), ())), preferred_element_type=F32
        )
        re, im = both[:kx], both[kx:]
        first = jnp.where(low, re, swap_halves(im))
        second = jnp.where(low, swap_halves(re), im)
        sect[2 * i] = first
        sect_s[2 * i] = swap_halves(first) * sgn_f
        sect[2 * i + 1] = second
        sect_s[2 * i + 1] = swap_halves(second) * sgn_f
        return carry

    lax.fori_loop(0, yd * td // 2, x_step, 0)

    pl.semaphore_wait(barrier, rows - 1 + slabs - 1 + 1)
    pending = []

    def send(src, dst, send_sem, recv_sem, target):
        copy = pltpu.make_async_remote_copy(
            src_ref=src,
            dst_ref=dst,
            send_sem=send_sem,
            recv_sem=recv_sem,
            device_id=target,
            device_id_type=MESH,
        )
        copy.start()
        pending.append(copy)
        return copy

    y_copies = []
    for c in range(count):
        arriving = []
        for d in list(range(1, rows)) + [0]:
            dest = lax.rem(row + d, rows)

            def y_step(a, carry, d=d, dest=dest):
                k = dest * kyd + a
                for t in range(td):
                    total = jnp.zeros((kx, 128), F32)
                    for y in range(yd):
                        total += tab_y[k, y0 + y] * sect[y * td + t]
                        total += tab_y[ky_all + k, y0 + y] * sect_s[y * td + t]
                    if d == 0:
                        y_recv[row, a, t] = total.astype(BF16)
                    else:
                        y_send[d - 1, a, t] = total.astype(BF16)
                return carry

            lax.fori_loop(c * span, (c + 1) * span, y_step, 0)
            if d > 0:
                arriving.append(
                    send(
                        y_send.at[d - 1, part[c]],
                        y_recv.at[row, part[c]],
                        ys_sem.at[d - 1, c],
                        yr_sem.at[d - 1, c],
                        {"row": dest},
                    )
                )
        y_copies.append(arriving)

    f_copy = send(field, f_all.at[:, mine, :], fs_sem, fr_sem, {"chan": 1 - chan})
    f_copy.wait_recv()

    eye = lax.broadcasted_iota(jnp.int32, (half, half), 0) == lax.broadcasted_iota(
        jnp.int32, (half, half), 1
    )
    column = jnp.sum(jnp.where(eye, bias[...], 0.0), axis=1, keepdims=True)

    def conv_step(i, carry):
        conv[i] = jnp.dot(conv_w[...], f_all[i], preferred_element_type=F32) + column
        return carry

    lax.fori_loop(0, yd * td, conv_step, 0)

    t_copies, c_copies, m_copies, b_copies = [], [], [], []

    def time_part(c):
        for copy in y_copies[c]:
            copy.wait_recv()

        def t_step(a, carry):
            parts = []
            for t in range(td):
                total = y_recv[0, a, t].astype(F32)
                for r in range(1, rows):
                    total += y_recv[r, a, t].astype(F32)
                parts.append((total, swap_halves(total) * sgn_f))
            for d in range(slabs):
                dest = lax.rem(tm + d, slabs)
                for b in range(ktd):
                    k = dest * ktd + b
                    value = jnp.zeros((kx, 128), F32)
                    for t in range(td):
                        value += tab_t[k, t0 + t] * parts[t][0]
                        value += tab_t[kt_all + k, t0 + t] * parts[t][1]
                    if d == 0:
                        own_kt[a, b] = value
                    else:
                        t_send[d - 1, a, b] = value.astype(BF16)
            return carry

        lax.fori_loop(c * span, (c + 1) * span, t_step, 0)
        t_copies.append(
            [
                send(
                    t_send.at[d - 1, part[c]],
                    t_recv.at[d - 1, part[c]],
                    ts_sem.at[d - 1, c],
                    tr_sem.at[d - 1, c],
                    {"tm": lax.rem(tm + d, slabs)},
                )
                for d in range(1, slabs)
            ]
        )

    def coef_part(c):
        for copy in t_copies[c]:
            copy.wait_recv()

        def c_step(a, carry):
            for b in range(ktd):
                value = own_kt[a, b]
                for d in range(1, slabs):
                    value += t_recv[d - 1, a, b].astype(F32)
                coef[chan, a, b] = value.astype(BF16)
            return carry

        lax.fori_loop(c * span, (c + 1) * span, c_step, 0)
        c_copies.append(
            send(
                coef.at[chan, part[c]],
                coef.at[chan, part[c]],
                cs_sem.at[c],
                cr_sem.at[c],
                {"chan": 1 - chan},
            )
        )

    group = 8 * 2 * half
    sub = lax.broadcasted_iota(jnp.int32, (8, 128), 0)
    zero = jnp.zeros((8, 128), F32)

    def mix_part(c):
        c_copies[c].wait_recv()
        w_copies[c].wait()

        def mix_step(i, carry):
            a, b = c * span + i // ktd, lax.rem(i, ktd)
            left = coef[0, a, b].astype(F32)
            right = coef[1, a, b].astype(F32)
            re = jnp.where(low, left, swap_halves(right))
            im = jnp.where(low, swap_halves(left), right)
            pieces = []
            for g in range(0, kx // 8, 2):
                first, second = slice(8 * g, 8 * g + 8), slice(8 * g + 8, 8 * g + 16)
                lhs = jnp.concatenate(
                    [
                        jnp.concatenate([re[first], zero], axis=1),
                        jnp.concatenate([im[first], zero], axis=1),
                        jnp.concatenate([zero, re[second]], axis=1),
                        jnp.concatenate([zero, im[second]], axis=1),
                    ],
                    axis=0,
                ).astype(BF16)
                rhs = jnp.concatenate(
                    [
                        w_all[b, a, g * group : (g + 1) * group, :],
                        w_all[b, a, (g + 1) * group : (g + 2) * group, :],
                    ],
                    axis=1,
                )
                result = lax.dot_general(
                    lhs, rhs, (((1,), (1,)), ((), ())), preferred_element_type=F32
                )
                for h in range(2):
                    by_part = []
                    for p in range(2):
                        tile = result[16 * h + 8 * p : 16 * h + 8 * p + 8]
                        total = tile[:, :128]
                        for m in range(1, 8):
                            total = jnp.where(sub == m, tile[:, 128 * m : 128 * m + 128], total)
                        by_part.append(total)
                    turned = swap_halves(by_part[1])
                    pieces.append(by_part[0] + jnp.where(low8, -turned, turned))
            modes[a, tm * ktd + b] = jnp.concatenate(pieces, axis=0).astype(BF16)
            return carry

        lax.fori_loop(0, span * ktd, mix_step, 0)
        own = pl.ds(tm * ktd, ktd)
        m_copies.append(
            [
                send(
                    modes.at[part[c], own],
                    modes.at[part[c], own],
                    ms_sem.at[d - 1, c],
                    mr_sem.at[d - 1, c],
                    {"tm": lax.rem(tm + d, slabs)},
                )
                for d in range(1, slabs)
            ]
        )

    def back_part(c):
        for copy in m_copies[c]:
            copy.wait_recv()

        def bt_step(a, carry):
            totals = [jnp.zeros((kx, 128), F32) for _ in range(td)]
            for k in range(kt_all):
                value = modes[a, k].astype(F32)
                turned = swap_halves(value) * sgn_b
                for t in range(td):
                    totals[t] += tab_t[k, t0 + t] * value + tab_t[kt_all + k, t0 + t] * turned
            for t in range(td):
                back[row, a, t] = totals[t].astype(BF16)
            return carry

        lax.fori_loop(c * span, (c + 1) * span, bt_step, 0)
        b_copies.append(
            [
                send(
                    back.at[row, part[c]],
                    back.at[row, part[c]],
                    bs_sem.at[d - 1, c],
                    br_sem.at[d - 1, c],
                    {"row": lax.rem(row + d, rows)},
                )
                for d in range(1, rows)
            ]
        )

    for c in range(count + 1):
        if c < count:
            time_part(c)
        if c > 0:
            mix_part(c - 1)
        if c < count:
            coef_part(c)
        if c > 0:
            back_part(c - 1)

    for c in range(count):
        for copy in b_copies[c]:
            copy.wait_recv()

        def by_step(t, carry, c=c):
            if c == 0:
                totals = [jnp.zeros((kx, 128), F32) for _ in range(yd)]
            else:
                totals = [acc[y * td + t] for y in range(yd)]
            for source in range(rows):
                for a in range(c * span, (c + 1) * span):
                    k = source * kyd + a
                    value = back[source, a, t].astype(F32)
                    turned = swap_halves(value) * sgn_b
                    for y in range(yd):
                        totals[y] += (
                            tab_y[k, y0 + y] * value + tab_y[ky_all + k, y0 + y] * turned
                        )
            for y in range(yd):
                acc[y * td + t] = totals[y]
            return carry

        lax.fori_loop(0, td, by_step, 0)

    def out_step(i, carry):
        first, second = acc[2 * i], acc[2 * i + 1]
        both = jnp.concatenate(
            [
                jnp.where(low, first, swap_halves(second)),
                jnp.where(low, swap_halves(first), second),
            ],
            axis=0,
        )
        spectral = jnp.dot(both.T.astype(BF16), x_inv[...], preferred_element_type=F32)
        value = spectral + conv[pl.ds(2 * i, 2)].reshape(2 * half, 128)
        value = 0.5 * value * (1.0 + lax.erf(value * np.float32(1.0 / np.sqrt(2.0))))
        out[pl.ds(2 * i, 2)] = value.astype(BF16).reshape(2, half, 128)
        return carry

    lax.fori_loop(0, yd * td // 2, out_step, 0)
    for copy in pending:
        copy.wait_send()


def body(field_in, spectral_weight, conv_weight, conv_bias):
    yd, td, half, nx = field_in.shape
    ktd, kyd, kx = spectral_weight.shape[:3]
    out_c, in_c = spectral_weight.shape[4:]
    rows, slabs = lax.axis_size("row"), lax.axis_size("tm")
    ny, nt = yd * rows, td * slabs
    ky_all, kt_all = kyd * rows, ktd * slabs

    turn_x = angles(np.arange(kx), np.arange(nx), nx)
    x_fwd = jnp.asarray(np.concatenate([np.cos(turn_x), -np.sin(turn_x)], axis=0), BF16)
    scale = (np.where(np.arange(kx) == 0, 1.0, 2.0) / (nx * ny * nt))[:, None]
    x_inv = jnp.asarray(
        np.concatenate([np.cos(turn_x) * scale, -np.sin(turn_x) * scale], axis=0), BF16
    )
    turn_y = angles(signed(ky_all), np.arange(ny), ny)
    tab_y = jnp.asarray(np.concatenate([np.cos(turn_y), np.sin(turn_y)], axis=0), F32)
    turn_t = angles(signed(kt_all), np.arange(nt), nt)
    tab_t = jnp.asarray(np.concatenate([np.cos(turn_t), np.sin(turn_t)], axis=0), F32)

    parts = min(4, kyd)
    dims = (rows, slabs, yd, td, kyd, ktd, kx, parts)
    vmem = pl.BlockSpec(memory_space=pltpu.VMEM)
    smem = pl.BlockSpec(memory_space=pltpu.SMEM)
    hbm = pl.BlockSpec(memory_space=pl.ANY)
    dma = pltpu.SemaphoreType.DMA
    tile = (kx, 128)
    result = pl.pallas_call(
        functools.partial(kernel, dims),
        out_shape=jax.ShapeDtypeStruct((yd * td, half, nx), BF16),
        in_specs=[hbm, hbm, vmem, vmem, vmem, vmem, smem, smem],
        out_specs=vmem,
        scratch_shapes=[
            pltpu.VMEM((ktd, kyd, kx * 2 * out_c, in_c), BF16),
            pltpu.VMEM((yd * td, in_c, nx), BF16),
            pltpu.VMEM((yd * td,) + tile, F32),
            pltpu.VMEM((yd * td,) + tile, F32),
            pltpu.VMEM((rows - 1, kyd, td) + tile, BF16),
            pltpu.VMEM((rows, kyd, td) + tile, BF16),
            pltpu.VMEM((kyd, ktd) + tile, F32),
            pltpu.VMEM((slabs - 1, kyd, ktd) + tile, BF16),
            pltpu.VMEM((slabs - 1, kyd, ktd) + tile, BF16),
            pltpu.VMEM((2, kyd, ktd) + tile, BF16),
            pltpu.VMEM((kyd, kt_all) + tile, BF16),
            pltpu.VMEM((rows, kyd, td) + tile, BF16),
            pltpu.VMEM((yd * td,) + tile, F32),
            pltpu.VMEM((yd * td, out_c, nx), F32),
            dma((parts,)),
            dma,
            dma,
            dma,
            dma((rows - 1, parts)),
            dma((rows - 1, parts)),
            dma((slabs - 1, parts)),
            dma((slabs - 1, parts)),
            dma((parts,)),
            dma((parts,)),
            dma((slabs - 1, parts)),
            dma((slabs - 1, parts)),
            dma((rows - 1, parts)),
            dma((rows - 1, parts)),
        ],
        compiler_params=pltpu.CompilerParams(
            collective_id=0, has_side_effects=True, vmem_limit_bytes=56 * 1024 * 1024
        ),
    )(
        field_in.reshape(yd * td, half, nx),
        spectral_weight.reshape(ktd, kyd, kx * 2 * out_c, in_c),
        conv_weight,
        conv_bias[None, :],
        x_fwd,
        x_inv,
        tab_y,
        tab_t,
    )
    return result.reshape(yd, td, half, nx)


def solution(mesh):
    return jax.shard_map(
        body,
        mesh=mesh,
        in_specs=(
            P(("groups", "row"), "tm", "chan", None),
            P("tm", "row", None, None, "chan", None),
            P("chan", None),
            P("chan"),
        ),
        out_specs=P(("groups", "row"), "tm", "chan", None),
        check_vma=False,
    )
```

```python
import functools

import jax
import jax.numpy as jnp
import numpy as np
from jax import lax
from jax.experimental import pallas as pl
from jax.experimental.pallas import tpu as pltpu
from jax.sharding import PartitionSpec as P

MESH = pl.DeviceIdType.MESH
F32 = jnp.float32
BF16 = jnp.bfloat16


def angles(frequency, position, period):
    return 2.0 * np.pi * np.mod(np.outer(frequency, position), period) / period


def signed(count):
    index = np.arange(count)
    return np.where(index < count // 2, index, index - count)


def swap_halves(value):
    return pltpu.roll(value, 64, axis=value.ndim - 1)


def kernel(
    dims,
    field,
    weights,
    conv_w,
    bias,
    x_fwd,
    x_inv,
    tab_y,
    tab_t,
    out,
    w_all,
    f_all,
    sect,
    sect_s,
    y_send,
    y_recv,
    own_kt,
    t_send,
    t_recv,
    coef,
    modes,
    back,
    acc,
    conv,
    w_sem,
    f_sem,
    fs_sem,
    fr_sem,
    ys_sem,
    yr_sem,
    ts_sem,
    tr_sem,
    cs_sem,
    cr_sem,
    ms_sem,
    mr_sem,
    bs_sem,
    br_sem,
):
    rows, slabs, yd, td, kyd, ktd, kx, parts = dims
    ky_all, kt_all = rows * kyd, slabs * ktd
    row, tm, chan = lax.axis_index("row"), lax.axis_index("tm"), lax.axis_index("chan")
    y0, t0 = row * yd, tm * td
    half = 64

    barrier = pltpu.get_barrier_semaphore()
    for d in range(1, rows):
        pl.semaphore_signal(
            barrier, inc=1, device_id={"row": lax.rem(row + d, rows)}, device_id_type=MESH
        )
    for d in range(1, slabs):
        pl.semaphore_signal(
            barrier, inc=1, device_id={"tm": lax.rem(tm + d, slabs)}, device_id_type=MESH
        )
    pl.semaphore_signal(barrier, inc=1, device_id={"chan": 1 - chan}, device_id_type=MESH)

    mine = pl.ds(pl.multiple_of(chan * half, half), half)
    own_field = pltpu.make_async_copy(field, f_all.at[:, mine, :], f_sem)
    own_field.start()
    span = max(1, kyd // parts)
    count = kyd // span
    part = [pl.ds(c * span, span) for c in range(count)]
    w_copies = [
        pltpu.make_async_copy(weights.at[:, part[c]], w_all.at[:, part[c]], w_sem.at[c])
        for c in range(count)
    ]
    for copy in w_copies:
        copy.start()

    lane = lax.broadcasted_iota(jnp.int32, (kx, 128), 1)
    low = lane < half
    sgn_f = jnp.where(low, 1.0, -1.0).astype(F32)
    low8 = low[:8]
    sgn_b = -sgn_f

    own_field.wait()

    def x_step(i, carry):
        block = f_all[pl.ds(2 * i, 2), mine, :].reshape(2 * half, 128)
        both = lax.dot_general(
            x_fwd[...], block, (((1,), (1,)), ((), ())), preferred_element_type=F32
        )
        re, im = both[:kx], both[kx:]
        first = jnp.where(low, re, swap_halves(im))
        second = jnp.where(low, swap_halves(re), im)
        sect[2 * i] = first
        sect_s[2 * i] = swap_halves(first) * sgn_f
        sect[2 * i + 1] = second
        sect_s[2 * i + 1] = swap_halves(second) * sgn_f
        return carry

    lax.fori_loop(0, yd * td // 2, x_step, 0, unroll=4)

    pl.semaphore_wait(barrier, rows - 1 + slabs - 1 + 1)
    pending = []

    def send(src, dst, send_sem, recv_sem, target):
        copy = pltpu.make_async_remote_copy(
            src_ref=src,
            dst_ref=dst,
            send_sem=send_sem,
            recv_sem=recv_sem,
            device_id=target,
            device_id_type=MESH,
        )
        copy.start()
        pending.append(copy)
        return copy

    y_copies = []
    for c in range(count):
        arriving = []
        for d in list(range(1, rows)) + [0]:
            dest = lax.rem(row + d, rows)

            def y_step(a, carry, d=d, dest=dest):
                k = dest * kyd + a
                for t in range(td):
                    total = jnp.zeros((kx, 128), F32)
                    for y in range(yd):
                        total += tab_y[k, y0 + y] * sect[y * td + t]
                        total += tab_y[ky_all + k, y0 + y] * sect_s[y * td + t]
                    if d == 0:
                        y_recv[row, a, t] = total.astype(BF16)
                    else:
                        y_send[d - 1, a, t] = total.astype(BF16)
                return carry

            lax.fori_loop(c * span, (c + 1) * span, y_step, 0)
            if d > 0:
                arriving.append(
                    send(
                        y_send.at[d - 1, part[c]],
                        y_recv.at[row, part[c]],
                        ys_sem.at[d - 1, c],
                        yr_sem.at[d - 1, c],
                        {"row": dest},
                    )
                )
        y_copies.append(arriving)

    f_copy = send(field, f_all.at[:, mine, :], fs_sem, fr_sem, {"chan": 1 - chan})
    f_copy.wait_recv()

    eye = lax.broadcasted_iota(jnp.int32, (half, half), 0) == lax.broadcasted_iota(
        jnp.int32, (half, half), 1
    )
    column = jnp.sum(jnp.where(eye, bias[...], 0.0), axis=1, keepdims=True)

    def conv_step(i, carry):
        conv[i] = jnp.dot(conv_w[...], f_all[i], preferred_element_type=F32) + column
        return carry

    lax.fori_loop(0, yd * td, conv_step, 0, unroll=4)

    t_copies, c_copies, m_copies, b_copies = [], [], [], []

    def time_part(c):
        for copy in y_copies[c]:
            copy.wait_recv()

        def t_step(a, carry):
            parts = []
            for t in range(td):
                total = y_recv[0, a, t].astype(F32)
                for r in range(1, rows):
                    total += y_recv[r, a, t].astype(F32)
                parts.append((total, swap_halves(total) * sgn_f))
            for d in range(slabs):
                dest = lax.rem(tm + d, slabs)
                for b in range(ktd):
                    k = dest * ktd + b
                    value = jnp.zeros((kx, 128), F32)
                    for t in range(td):
                        value += tab_t[k, t0 + t] * parts[t][0]
                        value += tab_t[kt_all + k, t0 + t] * parts[t][1]
                    if d == 0:
                        own_kt[a, b] = value
                    else:
                        t_send[d - 1, a, b] = value.astype(BF16)
            return carry

        lax.fori_loop(c * span, (c + 1) * span, t_step, 0)
        t_copies.append(
            [
                send(
                    t_send.at[d - 1, part[c]],
                    t_recv.at[d - 1, part[c]],
                    ts_sem.at[d - 1, c],
                    tr_sem.at[d - 1, c],
                    {"tm": lax.rem(tm + d, slabs)},
                )
                for d in range(1, slabs)
            ]
        )

    def coef_part(c):
        for copy in t_copies[c]:
            copy.wait_recv()

        def c_step(a, carry):
            for b in range(ktd):
                value = own_kt[a, b]
                for d in range(1, slabs):
                    value += t_recv[d - 1, a, b].astype(F32)
                coef[chan, a, b] = value.astype(BF16)
            return carry

        lax.fori_loop(c * span, (c + 1) * span, c_step, 0)
        c_copies.append(
            send(
                coef.at[chan, part[c]],
                coef.at[chan, part[c]],
                cs_sem.at[c],
                cr_sem.at[c],
                {"chan": 1 - chan},
            )
        )

    group = 8 * 2 * half
    sub = lax.broadcasted_iota(jnp.int32, (8, 128), 0)
    zero = jnp.zeros((8, 128), F32)

    def mix_part(c):
        c_copies[c].wait_recv()
        w_copies[c].wait()

        def mix_step(i, carry):
            a, b = c * span + i // ktd, lax.rem(i, ktd)
            left = coef[0, a, b].astype(F32)
            right = coef[1, a, b].astype(F32)
            re = jnp.where(low, left, swap_halves(right))
            im = jnp.where(low, swap_halves(left), right)
            pieces = []
            for g in range(0, kx // 8, 2):
                first, second = slice(8 * g, 8 * g + 8), slice(8 * g + 8, 8 * g + 16)
                lhs = jnp.concatenate(
                    [
                        jnp.concatenate([re[first], zero], axis=1),
                        jnp.concatenate([im[first], zero], axis=1),
                        jnp.concatenate([zero, re[second]], axis=1),
                        jnp.concatenate([zero, im[second]], axis=1),
                    ],
                    axis=0,
                ).astype(BF16)
                rhs = jnp.concatenate(
                    [
                        w_all[b, a, g * group : (g + 1) * group, :],
                        w_all[b, a, (g + 1) * group : (g + 2) * group, :],
                    ],
                    axis=1,
                )
                result = lax.dot_general(
                    lhs, rhs, (((1,), (1,)), ((), ())), preferred_element_type=F32
                )
                for h in range(2):
                    by_part = []
                    for p in range(2):
                        tile = result[16 * h + 8 * p : 16 * h + 8 * p + 8]
                        total = tile[:, :128]
                        for m in range(1, 8):
                            total = jnp.where(sub == m, tile[:, 128 * m : 128 * m + 128], total)
                        by_part.append(total)
                    turned = swap_halves(by_part[1])
                    pieces.append(by_part[0] + jnp.where(low8, -turned, turned))
            modes[a, tm * ktd + b] = jnp.concatenate(pieces, axis=0).astype(BF16)
            return carry

        lax.fori_loop(0, span * ktd, mix_step, 0, unroll=2)
        own = pl.ds(tm * ktd, ktd)
        m_copies.append(
            [
                send(
                    modes.at[part[c], own],
                    modes.at[part[c], own],
                    ms_sem.at[d - 1, c],
                    mr_sem.at[d - 1, c],
                    {"tm": lax.rem(tm + d, slabs)},
                )
                for d in range(1, slabs)
            ]
        )

    def back_part(c):
        for copy in m_copies[c]:
            copy.wait_recv()

        def bt_step(a, carry):
            totals = [jnp.zeros((kx, 128), F32) for _ in range(td)]
            for k in range(kt_all):
                value = modes[a, k].astype(F32)
                turned = swap_halves(value) * sgn_b
                for t in range(td):
                    totals[t] += tab_t[k, t0 + t] * value + tab_t[kt_all + k, t0 + t] * turned
            for t in range(td):
                back[row, a, t] = totals[t].astype(BF16)
            return carry

        lax.fori_loop(c * span, (c + 1) * span, bt_step, 0)
        b_copies.append(
            [
                send(
                    back.at[row, part[c]],
                    back.at[row, part[c]],
                    bs_sem.at[d - 1, c],
                    br_sem.at[d - 1, c],
                    {"row": lax.rem(row + d, rows)},
                )
                for d in range(1, rows)
            ]
        )

    for c in range(count + 1):
        if c < count:
            time_part(c)
        if c > 0:
            mix_part(c - 1)
        if c < count:
            coef_part(c)
        if c > 0:
            back_part(c - 1)

    for c in range(count):
        for copy in b_copies[c]:
            copy.wait_recv()

        def by_step(t, carry, c=c):
            if c == 0:
                totals = [jnp.zeros((kx, 128), F32) for _ in range(yd)]
            else:
                totals = [acc[y * td + t] for y in range(yd)]
            for source in range(rows):
                for a in range(c * span, (c + 1) * span):
                    k = source * kyd + a
                    value = back[source, a, t].astype(F32)
                    turned = swap_halves(value) * sgn_b
                    for y in range(yd):
                        totals[y] += (
                            tab_y[k, y0 + y] * value + tab_y[ky_all + k, y0 + y] * turned
                        )
            for y in range(yd):
                acc[y * td + t] = totals[y]
            return carry

        lax.fori_loop(0, td, by_step, 0)

    def out_step(i, carry):
        first, second = acc[2 * i], acc[2 * i + 1]
        both = jnp.concatenate(
            [
                jnp.where(low, first, swap_halves(second)),
                jnp.where(low, swap_halves(first), second),
            ],
            axis=0,
        )
        spectral = jnp.dot(both.T.astype(BF16), x_inv[...], preferred_element_type=F32)
        value = spectral + conv[pl.ds(2 * i, 2)].reshape(2 * half, 128)
        value = 0.5 * value * (1.0 + lax.erf(value * np.float32(1.0 / np.sqrt(2.0))))
        out[pl.ds(2 * i, 2)] = value.astype(BF16).reshape(2, half, 128)
        return carry

    lax.fori_loop(0, yd * td // 2, out_step, 0, unroll=4)
    for copy in pending:
        copy.wait_send()


def body(field_in, spectral_weight, conv_weight, conv_bias):
    yd, td, half, nx = field_in.shape
    ktd, kyd, kx = spectral_weight.shape[:3]
    out_c, in_c = spectral_weight.shape[4:]
    rows, slabs = lax.axis_size("row"), lax.axis_size("tm")
    ny, nt = yd * rows, td * slabs
    ky_all, kt_all = kyd * rows, ktd * slabs

    turn_x = angles(np.arange(kx), np.arange(nx), nx)
    x_fwd = jnp.asarray(np.concatenate([np.cos(turn_x), -np.sin(turn_x)], axis=0), BF16)
    scale = (np.where(np.arange(kx) == 0, 1.0, 2.0) / (nx * ny * nt))[:, None]
    x_inv = jnp.asarray(
        np.concatenate([np.cos(turn_x) * scale, -np.sin(turn_x) * scale], axis=0), BF16
    )
    turn_y = angles(signed(ky_all), np.arange(ny), ny)
    tab_y = jnp.asarray(np.concatenate([np.cos(turn_y), np.sin(turn_y)], axis=0), F32)
    turn_t = angles(signed(kt_all), np.arange(nt), nt)
    tab_t = jnp.asarray(np.concatenate([np.cos(turn_t), np.sin(turn_t)], axis=0), F32)

    parts = min(4, kyd)
    dims = (rows, slabs, yd, td, kyd, ktd, kx, parts)
    vmem = pl.BlockSpec(memory_space=pltpu.VMEM)
    smem = pl.BlockSpec(memory_space=pltpu.SMEM)
    hbm = pl.BlockSpec(memory_space=pl.ANY)
    dma = pltpu.SemaphoreType.DMA
    tile = (kx, 128)
    result = pl.pallas_call(
        functools.partial(kernel, dims),
        out_shape=jax.ShapeDtypeStruct((yd * td, half, nx), BF16),
        in_specs=[hbm, hbm, vmem, vmem, vmem, vmem, smem, smem],
        out_specs=vmem,
        scratch_shapes=[
            pltpu.VMEM((ktd, kyd, kx * 2 * out_c, in_c), BF16),
            pltpu.VMEM((yd * td, in_c, nx), BF16),
            pltpu.VMEM((yd * td,) + tile, F32),
            pltpu.VMEM((yd * td,) + tile, F32),
            pltpu.VMEM((rows - 1, kyd, td) + tile, BF16),
            pltpu.VMEM((rows, kyd, td) + tile, BF16),
            pltpu.VMEM((kyd, ktd) + tile, F32),
            pltpu.VMEM((slabs - 1, kyd, ktd) + tile, BF16),
            pltpu.VMEM((slabs - 1, kyd, ktd) + tile, BF16),
            pltpu.VMEM((2, kyd, ktd) + tile, BF16),
            pltpu.VMEM((kyd, kt_all) + tile, BF16),
            pltpu.VMEM((rows, kyd, td) + tile, BF16),
            pltpu.VMEM((yd * td,) + tile, F32),
            pltpu.VMEM((yd * td, out_c, nx), F32),
            dma((parts,)),
            dma,
            dma,
            dma,
            dma((rows - 1, parts)),
            dma((rows - 1, parts)),
            dma((slabs - 1, parts)),
            dma((slabs - 1, parts)),
            dma((parts,)),
            dma((parts,)),
            dma((slabs - 1, parts)),
            dma((slabs - 1, parts)),
            dma((rows - 1, parts)),
            dma((rows - 1, parts)),
        ],
        compiler_params=pltpu.CompilerParams(
            collective_id=0, has_side_effects=True, vmem_limit_bytes=56 * 1024 * 1024
        ),
    )(
        field_in.reshape(yd * td, half, nx),
        spectral_weight.reshape(ktd, kyd, kx * 2 * out_c, in_c),
        conv_weight,
        conv_bias[None, :],
        x_fwd,
        x_inv,
        tab_y,
        tab_t,
    )
    return result.reshape(yd, td, half, nx)


def solution(mesh):
    return jax.shard_map(
        body,
        mesh=mesh,
        in_specs=(
            P(("groups", "row"), "tm", "chan", None),
            P("tm", "row", None, None, "chan", None),
            P("chan", None),
            P("chan"),
        ),
        out_specs=P(("groups", "row"), "tm", "chan", None),
        check_vma=False,
    )
```
